32 devices in a mesh: energy: 8 (over z, y), transpor: 4 (over x, core).
Axes of the slice: x: 2, y: 2, z: 4, core: 2. Of those that a mesh axis runs over, the one named last changes fastest.
Arguments:
- ham_diag: float32 [8, 2, 192, 192], P('transpor'), may hold values from -1 to 1, as said below
- ham_hop: float32 [8, 2, 192, 192], P('transpor'), may hold values from -1.3 to 1.3, as said below
- inject: float32 [8, 2, 192, 192], P('transpor'), may hold values from -4 to 4
- chemical: float32 [192], replicated, may hold values from -1 to 1
- energy_slot: int32 [8], P('energy'), may hold values from 0 to 7, each once
- onsite_shift: float32 [8, 8, 192], P('energy', 'transpor'), may hold values from -3 to 3
- onsite_loss: float32 [8, 8, 192], P('energy', 'transpor'), may hold values from 0.05 to 0.4
Outputs:
- polar: float32 [8, 8, 2, 192, 192], P('energy', 'transpor')
The draws below stay inside these ranges and needn't reach their ends.
Inputs may be any that keep to these rules, and one draw needn't show every extreme that they name: `energy_slot`: every grid index 0 to 7 appears once. `ham_diag`: each block is Hermitian: real part symmetric, imaginary part antisymmetric. `ham_hop`: the diagonal of each block has real parts of 0.7 to 1.3 and imaginary parts 0.
All inputs are finite; a program needn't handle non-finite values.
Results may differ from the reference program's by a relative error of at most 0.0003.
Values sent between devices are 32-bit elements; how exact they have to be, the bound alone decides.
A program may use at most 128 MiB of HBM per device.

```python
import math
import jax
import jax.numpy as jnp
from jax import lax

M = 192
R = 192
NB = 8
NE = 8


def draw_ham_diag(key, part):
    key = jax.random.fold_in(key, 5)
    key_off, key_site = jax.random.split(key)
    spread = 0.5 / math.sqrt(M)
    raw_values = jax.random.normal(key_off, (NB, 2, M, M), jnp.float32) * spread
    raw_values = jnp.clip(raw_values, -0.35, 0.35)
    identity = jnp.eye(M, dtype=jnp.float32)
    sym_part = (raw_values[:, 0] + jnp.swapaxes(raw_values[:, 0], 1, 2)) * 0.7071 * (1.0 - identity)
    anti_part = (raw_values[:, 1] - jnp.swapaxes(raw_values[:, 1], 1, 2)) * 0.7071
    onsite = jax.random.uniform(key_site, (NB, M), jnp.float32, -1.0, 1.0)
    real_part = sym_part + onsite[:, :, None] * identity
    return jnp.stack([real_part, anti_part], axis=1)


def draw_ham_hop(key, part):
    key = jax.random.fold_in(key, 9)
    key_off, key_site = jax.random.split(key)
    spread = 0.4 / math.sqrt(M)
    raw_values = jax.random.normal(key_off, (NB, 2, M, M), jnp.float32) * spread
    raw_values = jnp.clip(raw_values, -0.6, 0.6)
    identity = jnp.eye(M, dtype=jnp.float32)
    raw_values = raw_values * (1.0 - identity)
    hopping = jax.random.uniform(key_site, (NB, M), jnp.float32, 0.7, 1.3)
    real_part = raw_values[:, 0] + hopping[:, :, None] * identity
    return jnp.stack([real_part, raw_values[:, 1]], axis=1)


def block_levels(stream_key, extent, cuts, least, high):
    level, own = 1.0, jax.random.fold_in(stream_key, 6)
    for axis_at, parts in cuts:
        steps = jnp.exp(jax.random.uniform(jax.random.fold_in(own, axis_at), (parts,), jnp.float32, least / len(cuts), high / len(cuts)))
        level = level * jnp.repeat(steps, extent[axis_at] // parts).reshape([-1 if axis == axis_at else 1 for axis in range(len(extent))])
    return level


def bell_draw(key, extent, width, limit, cuts=(), held_as=jnp.bfloat16):
    values = jax.random.normal(key, extent, jnp.float32) * width
    if len(cuts) > 0:
        values = block_levels(key, extent, cuts, -0.22, 0.18) * values
    return jnp.clip(values, min=-limit, max=limit).astype(held_as)


def setup_inputs(seed: int = 0) -> dict:
    key_of = jax.random.split(jax.random.key(seed), 8)
    ham_diag = draw_ham_diag(jax.random.fold_in(key_of[7], 71), 0)
    ham_hop = draw_ham_hop(jax.random.fold_in(key_of[7], 71), 0)
    inject = bell_draw(key_of[2], (NB, 2, M, R), 0.3, 4.0, ((0, 4),), jnp.float32)
    chemical = jnp.clip(jax.random.uniform(key_of[3], (R,), jnp.float32, -1.0, 1.0), -1.0, 1.0)
    energy_slot = jax.random.permutation(key_of[4], NE).astype(jnp.int32)
    onsite_shift = bell_draw(key_of[5], (NE, NB, M), 0.2, 3.0, ((0, 8), (1, 4)), jnp.float32)
    onsite_loss = jnp.clip(jnp.exp(math.log(0.4) - 2.0794415 * jax.random.uniform(key_of[6], (NE, NB, M), jnp.float32) ** block_levels(key_of[6], (NE, NB, M), ((0, 8), (1, 4)), -0.2, 0.2)), 0.05, 0.4)
    return dict(ham_diag=ham_diag, ham_hop=ham_hop, inject=inject, chemical=chemical, energy_slot=energy_slot, onsite_shift=onsite_shift, onsite_loss=onsite_loss)


ENERGY_LOW = -1.5
ENERGY_SPAN = 3.0
THERMAL = 0.1

def product_hi(left_op, right_op):
    return jnp.einsum('...ik,...kj->...ij', left_op, right_op, precision=lax.Precision.HIGHEST)

def complex_mul(left_op, right_op):
    left_re, left_im = (left_op[..., 0, :, :], left_op[..., 1, :, :])
    right_re, right_im = (right_op[..., 0, :, :], right_op[..., 1, :, :])
    real_part = product_hi(left_re, right_re) - product_hi(left_im, right_im)
    imag_part = product_hi(left_re, right_im) + product_hi(left_im, right_re)
    return jnp.stack([real_part, imag_part], axis=-3)

def complex_adj(matrix):
    return jnp.stack([jnp.swapaxes(matrix[..., 0, :, :], -1, -2), -jnp.swapaxes(matrix[..., 1, :, :], -1, -2)], axis=-3)

def complex_solve(matrix, right_side):
    real_part, imag_part = (matrix[0], matrix[1])
    expanded = jnp.concatenate([jnp.concatenate([real_part, -imag_part], 1), jnp.concatenate([imag_part, real_part], 1)], 0)
    stacked = jnp.concatenate([right_side[0], right_side[1]], 0)
    solved = jnp.linalg.solve(expanded, stacked)
    half_rows = matrix.shape[1]
    return jnp.stack([solved[:half_rows], solved[half_rows:]])

def diagonal_blocks(ham_diag, ham_hop, energy, shift_row, loss_row):
    identity = jnp.eye(M, dtype=jnp.float32)
    real_part = energy * identity - ham_diag[:, 0] - shift_row[:, :, None] * identity
    imag_part = -ham_diag[:, 1] + loss_row[:, :, None] * identity
    contact = complex_mul(ham_hop[-1], complex_adj(ham_hop[-1]))
    real_part = real_part.at[-1].add(-contact[1])
    imag_part = imag_part.at[-1].add(contact[0])
    return jnp.stack([real_part, imag_part], axis=1)

def chain_solve(blocks, ham_hop, inject):
    upper_all = -ham_hop
    lower_all = jnp.concatenate([jnp.zeros_like(ham_hop[:1]), -complex_adj(ham_hop[:-1])], 0)

    def forward(carried, items):
        prev_coupled, prev_partial = carried
        diag_blk, lower_blk, upper_blk, source = items
        schur_blk = diag_blk - complex_mul(lower_blk, prev_coupled)
        source = source - complex_mul(lower_blk, prev_partial)
        solved_pair = complex_solve(schur_blk, jnp.concatenate([upper_blk, source], 2))
        outputs = (solved_pair[:, :, :M], solved_pair[:, :, M:])
        return (outputs, outputs)
    initial = (jnp.zeros((2, M, M), jnp.float32), jnp.zeros((2, M, R), jnp.float32))
    unused_end, (coupled, partial_value) = lax.scan(forward, initial, (blocks, lower_all, upper_all, inject))

    def backward(carried, items):
        coupled_blk, partial_blk = items
        result = partial_blk - complex_mul(coupled_blk, carried)
        return (result, result)
    unused_first, states = lax.scan(backward, jnp.zeros((2, M, R), jnp.float32), (coupled, partial_value), reverse=True)
    return states

def density(states, weight):
    state_re, state_im = (states[:, 0], states[:, 1])
    weighted_re = state_re * weight[None, None, :]
    weighted_im = state_im * weight[None, None, :]
    high = lax.Precision.HIGHEST
    real_part = jnp.einsum('bir,bjr->bij', weighted_re, state_re, precision=high) + jnp.einsum('bir,bjr->bij', weighted_im, state_im, precision=high)
    imag_part = jnp.einsum('bir,bjr->bij', weighted_im, state_re, precision=high) - jnp.einsum('bir,bjr->bij', weighted_re, state_im, precision=high)
    return jnp.stack([real_part, imag_part], axis=1)

def reference(ham_diag, ham_hop, inject, chemical, energy_slot, onsite_shift, onsite_loss):

    def one_energy(items):
        slot_value, shift_row, loss_row = items
        energy = ENERGY_LOW + ENERGY_SPAN * (slot_value.astype(jnp.float32) + 0.5) / NE
        blocks = diagonal_blocks(ham_diag, ham_hop, energy, shift_row, loss_row)
        states = chain_solve(blocks, ham_hop, inject)
        occupied = 1.0 / (1.0 + jnp.exp((energy - chemical) / THERMAL))
        return (density(states, occupied), density(states, 1.0 - occupied))
    lesser, greater = lax.map(one_energy, (energy_slot, onsite_shift, onsite_loss))
    lesser = jnp.zeros_like(lesser).at[energy_slot].set(lesser)
    greater = jnp.zeros_like(greater).at[energy_slot].set(greater)
    padded = jnp.concatenate([jnp.zeros_like(greater), greater], 0)

    def one_lag(lag_value):
        moved = lax.dynamic_slice_in_dim(padded, (NE - lag_value).astype(jnp.int32), NE, 0)
        real_part = jnp.sum(lesser[:, :, 0] * moved[:, :, 0] + lesser[:, :, 1] * moved[:, :, 1], 0)
        imag_part = jnp.sum(lesser[:, :, 1] * moved[:, :, 0] - lesser[:, :, 0] * moved[:, :, 1], 0)
        return jnp.stack([real_part, imag_part], axis=1) / NE
    return lax.map(one_lag, jnp.arange(NE, dtype=jnp.int32))
```

```python
import functools
import math

import jax
import jax.numpy as jnp
from jax import lax
from jax.experimental import pallas as pl
from jax.experimental.pallas import tpu as pltpu
from jax.sharding import PartitionSpec as P

ENERGY_LOW = -1.5
ENERGY_SPAN = 3.0
THERMAL = 0.1
LOSS_FLOOR = 0.05


def dot_exact(left_op, right_op):
    return jnp.dot(
        left_op,
        right_op,
        precision=lax.Precision.HIGHEST,
        preferred_element_type=jnp.float32,
    )


def stacked_dot(left_stack, right_op):
    return dot_exact(left_stack, right_op)


def combine(with_re, with_im):
    rows = with_re.shape[0] // 2
    return with_re[:rows] - with_im[rows:], with_re[rows:] + with_im[:rows]


def cmul(left_op, right_op):
    left_stack = jnp.concatenate(left_op, axis=0)
    return combine(stacked_dot(left_stack, right_op[0]), stacked_dot(left_stack, right_op[1]))


def split(value):
    high = value.astype(jnp.bfloat16)
    return high, (value - high.astype(jnp.float32)).astype(jnp.bfloat16)


def three_term(left_stack, right_op):
    left_hi, left_lo = left_stack
    right_hi, right_lo = right_op
    rows = left_hi.shape[0]
    wide = jnp.dot(
        jnp.concatenate([left_hi, left_lo], axis=0), right_hi, preferred_element_type=jnp.float32
    )
    narrow = jnp.dot(left_hi, right_lo, preferred_element_type=jnp.float32)
    return wide[:rows] + (wide[rows:] + narrow)


def cmul_split(left_stack, right_op):
    return combine(three_term(left_stack, right_op[0]), three_term(left_stack, right_op[1]))


def stack_split(value):
    return split(jnp.concatenate(value, axis=0))


def invert(matrix_re, matrix_im, x_ref):
    start = (jnp.transpose(matrix_re), -jnp.transpose(matrix_im))
    matrix_stack = stack_split((matrix_re, matrix_im))
    x_ref[0] = start[0]
    x_ref[1] = start[1]
    gram = cmul_split(matrix_stack, (split(start[0]), split(start[1])))
    sums = jnp.sum(jnp.abs(gram[0]) + jnp.abs(gram[1]), axis=0, keepdims=True)
    high = jnp.max(sums)
    low = jnp.float32(0.98 * LOSS_FLOOR * LOSS_FLOOR)

    def step(x_re, x_im, product, scale):
        x_stack = stack_split((x_re, x_im))
        next_re, next_im = cmul_split(x_stack, (split(product[0]), split(product[1])))
        x_ref[0] = scale * (2.0 * x_re - scale * next_re)
        x_ref[1] = scale * (2.0 * x_im - scale * next_im)

    scale = 2.0 / (low + high)
    step(start[0], start[1], gram, scale)
    low = low * high * scale * scale

    def refine(low):
        x_re, x_im = x_ref[0], x_ref[1]
        product = cmul_split(matrix_stack, (split(x_re), split(x_im)))
        scale = 2.0 / (1.0 + low)
        step(x_re, x_im, product, scale)
        return low * scale * scale

    low = lax.while_loop(lambda low: low < 0.998, refine, low)
    scale = 2.0 / (1.0 + low)
    x_re, x_im = x_ref[0], x_ref[1]
    product = cmul((matrix_re, matrix_im), (x_re, x_im))
    last_re, last_im = cmul((x_re, x_im), product)
    return scale * (2.0 * x_re - scale * last_re), scale * (2.0 * x_im - scale * last_im)


def take(ref, first):
    return ref[first], ref[first + 1]


def put(ref, first, value):
    ref[first] = value[0]
    ref[first + 1] = value[1]


def minus(left_op, right_op):
    return left_op[0] - right_op[0], left_op[1] - right_op[1]


def eliminate_kernel(carry, diag_a, diag_b, low_a, up_a, low_b, up_b, src_a, src_b,
                     first_out, second_out, reduced_out, x_ref):
    pivot = minus(take(diag_a, 0), cmul(take(low_a, 0), take(carry, 0)))
    source = minus(take(src_a, 0), cmul(take(low_a, 0), take(carry, 2)))
    inverse = invert(pivot[0], pivot[1], x_ref)
    put(first_out, 0, cmul(inverse, take(up_a, 0)))
    put(first_out, 2, cmul(inverse, source))
    pivot = minus(take(diag_b, 0), cmul(take(low_b, 0), take(first_out, 0)))
    source = minus(take(src_b, 0), cmul(take(low_b, 0), take(first_out, 2)))
    put(reduced_out, 0, pivot)
    put(reduced_out, 2, source)
    inverse = invert(pivot[0], pivot[1], x_ref)
    put(second_out, 0, cmul(inverse, take(up_b, 0)))
    put(second_out, 2, cmul(inverse, source))


def join_kernel(carry, reduced, up_b, value_out, x_ref):
    pivot = minus(take(reduced, 0), cmul(take(up_b, 0), take(carry, 0)))
    source = minus(take(reduced, 2), cmul(take(up_b, 0), take(carry, 2)))
    inverse = invert(pivot[0], pivot[1], x_ref)
    put(value_out, 0, cmul(inverse, source))


def back_kernel(value, second, first, second_out, first_out):
    result = minus(take(second, 2), cmul(take(second, 0), take(value, 0)))
    put(second_out, 0, result)
    put(first_out, 0, minus(take(first, 2), cmul(take(first, 0), result)))


def back_first_kernel(value, first, first_out):
    put(first_out, 0, minus(take(first, 2), cmul(take(first, 0), take(value, 0))))


def call(body, counts, order, scratch=True):
    shapes = [jax.ShapeDtypeStruct((count, order, order), jnp.float32) for count in counts]
    return pl.pallas_call(
        body,
        out_shape=shapes,
        scratch_shapes=[pltpu.VMEM((2, order, order), jnp.float32)] if scratch else [],
        compiler_params=pltpu.CompilerParams(vmem_limit_bytes=48 * 1024 * 1024),
    )


def passed_along(x, axis, by):
    length = lax.axis_size(axis)
    pairs = [(i, i + by) for i in range(length) if 0 <= i + by < length]
    return lax.ppermute(x, axis, pairs)


def product_hi(left_op, right_op):
    return jnp.einsum("...ik,...kj->...ij", left_op, right_op, precision=lax.Precision.HIGHEST)


def complex_mul(left_op, right_op):
    left_re, left_im = (left_op[..., 0, :, :], left_op[..., 1, :, :])
    right_re, right_im = (right_op[..., 0, :, :], right_op[..., 1, :, :])
    real_part = product_hi(left_re, right_re) - product_hi(left_im, right_im)
    imag_part = product_hi(left_re, right_im) + product_hi(left_im, right_re)
    return jnp.stack([real_part, imag_part], axis=-3)


def complex_adj(matrix):
    return jnp.stack(
        [jnp.swapaxes(matrix[..., 0, :, :], -1, -2), -jnp.swapaxes(matrix[..., 1, :, :], -1, -2)],
        axis=-3,
    )


def per_device(ham_diag, ham_hop, inject, chemical, energy_slot, onsite_shift, onsite_loss):
    orbitals = ham_diag.shape[2]
    energies = energy_slot.shape[0]
    partitions = lax.axis_size("transpor")
    half = partitions // 2
    my_index = lax.axis_index("transpor")
    grid_total = energies * lax.axis_size("energy")
    high = lax.Precision.HIGHEST
    energy = ENERGY_LOW + ENERGY_SPAN * (energy_slot.astype(jnp.float32) + 0.5) / grid_total
    identity = jnp.eye(orbitals, dtype=jnp.float32)
    real_part = (
        energy[0] * identity - ham_diag[:, 0] - onsite_shift[0, :, :, None] * identity
    )
    imag_part = -ham_diag[:, 1] + onsite_loss[0, :, :, None] * identity
    contact = complex_mul(ham_hop[-1], complex_adj(ham_hop[-1]))
    is_last = (my_index == partitions - 1).astype(jnp.float32)
    real_part = real_part.at[-1].add(-is_last * contact[1])
    imag_part = imag_part.at[-1].add(is_last * contact[0])
    diag_blocks = jnp.stack([real_part, imag_part], axis=1)
    prev_hop = passed_along(ham_hop[-1], "transpor", 1)
    from_left = my_index < half

    def pick(left_op, right_op):
        return jnp.where(from_left, left_op, right_op)

    diag_a = pick(diag_blocks[0], diag_blocks[1])
    diag_b = pick(diag_blocks[1], diag_blocks[0])
    src_a = pick(inject[0], inject[1])
    src_b = pick(inject[1], inject[0])
    behind = -complex_adj(prev_hop)
    within = -complex_adj(ham_hop[0])
    low_a = pick(behind, -ham_hop[1])
    up_a = pick(-ham_hop[0], within)
    low_b = pick(within, -ham_hop[0])
    up_b = pick(-ham_hop[1], behind)

    carry = jnp.zeros((4, orbitals, orbitals), jnp.float32)
    kept = (carry, carry, carry)
    eliminate = call(eliminate_kernel, (4, 4, 4), orbitals)
    for stage in range(half):
        active = (my_index == stage) | (my_index == partitions - 1 - stage)
        kept = lax.cond(
            active,
            lambda now, then: tuple(
                eliminate(now, diag_a, diag_b, low_a, up_a, low_b, up_b, src_a, src_b)
            ),
            lambda now, then: then,
            carry,
            kept,
        )
        other = partitions - 1 - stage
        if stage < half - 1:
            pairs = [(stage, stage + 1), (other, other - 1)]
        else:
            pairs = [(stage, other), (other, stage)]
        carry = lax.ppermute(kept[1], "transpor", pairs)
    first, second, reduced = kept
    middle = (my_index == half - 1) | (my_index == half)
    (value_b,) = call(join_kernel, (2,), orbitals)(carry, reduced, up_b)
    (value_a,) = call(back_first_kernel, (2,), orbitals, False)(value_b, first)
    for stage in range(half - 2, -1, -1):
        other = partitions - 1 - stage
        passed = lax.ppermute(value_a, "transpor", [(stage + 1, stage), (other - 1, other)])
        new_b, new_a = call(back_kernel, (2, 2), orbitals, False)(passed, second, first)
        active = (my_index == stage) | (my_index == other)
        value_b = jnp.where(active, new_b, value_b)
        value_a = jnp.where(active, new_a, value_a)
    states = jnp.stack([pick(value_a, value_b), pick(value_b, value_a)])[None]
    occupied = 1.0 / (1.0 + jnp.exp((energy[:, None] - chemical[None, :]) / THERMAL))
    state_re = states[:, :, 0]
    state_im = states[:, :, 1]

    def density(weight):
        weighted_re = state_re * weight[:, None, None, :]
        weighted_im = state_im * weight[:, None, None, :]
        dens_re = jnp.einsum("ebir,ebjr->ebij", weighted_re, state_re, precision=high) + jnp.einsum(
            "ebir,ebjr->ebij", weighted_im, state_im, precision=high
        )
        dens_im = jnp.einsum("ebir,ebjr->ebij", weighted_im, state_re, precision=high) - jnp.einsum(
            "ebir,ebjr->ebij", weighted_re, state_im, precision=high
        )
        return jnp.stack([dens_re, dens_im], axis=2)

    lesser = density(occupied)
    greater = density(1.0 - occupied)
    all_slots = lax.all_gather(energy_slot, "energy", axis=0, tiled=True)
    span_len = 2 * grid_total
    frequency = lax.iota(jnp.int32, span_len)
    phase_in = frequency[:, None] * all_slots[None, :] % span_len
    angle_in = 2.0 * math.pi / span_len * phase_in.astype(jnp.float32)
    cos_in = jnp.cos(angle_in)
    sin_in = jnp.sin(angle_in)
    lag_index = lax.iota(jnp.int32, grid_total)
    phase_out = lag_index[:, None] * frequency[None, :] % span_len
    angle_out = 2.0 * math.pi / span_len * phase_out.astype(jnp.float32)
    cos_out = jnp.cos(angle_out)
    sin_out = jnp.sin(angle_out)
    lesser_x = lax.all_to_all(lesser, "energy", split_axis=3, concat_axis=0, tiled=True)
    greater_x = lax.all_to_all(greater, "energy", split_axis=3, concat_axis=0, tiled=True)
    piece_shape = lesser_x[:, :, 0].shape

    def transform(array):
        flat_re = array[:, :, 0].reshape(grid_total, -1)
        flat_im = array[:, :, 1].reshape(grid_total, -1)
        out_re = jnp.dot(cos_in, flat_re, precision=high) + jnp.dot(sin_in, flat_im, precision=high)
        out_im = jnp.dot(cos_in, flat_im, precision=high) - jnp.dot(sin_in, flat_re, precision=high)
        return (out_re, out_im)

    lesser_re, lesser_im = transform(lesser_x)
    greater_re, greater_im = transform(greater_x)
    prod_re = lesser_re * greater_re + lesser_im * greater_im
    prod_im = lesser_im * greater_re - lesser_re * greater_im
    scale = 1.0 / (span_len * grid_total)
    polar_re = (
        jnp.dot(cos_out, prod_re, precision=high) - jnp.dot(sin_out, prod_im, precision=high)
    ) * scale
    polar_im = (
        jnp.dot(cos_out, prod_im, precision=high) + jnp.dot(sin_out, prod_re, precision=high)
    ) * scale
    merged = jnp.stack([polar_re.reshape(piece_shape), polar_im.reshape(piece_shape)], axis=2)
    return lax.all_to_all(merged, "energy", split_axis=0, concat_axis=3, tiled=True)


def solution(mesh):
    in_specs = (
        P("transpor", None, None, None),
        P("transpor", None, None, None),
        P("transpor", None, None, None),
        P(),
        P("energy"),
        P("energy", "transpor", None),
        P("energy", "transpor", None),
    )
    out_specs = P("energy", "transpor", None, None, None)
    return jax.shard_map(
        per_device, mesh=mesh, in_specs=in_specs, out_specs=out_specs, check_vma=False
    )
```

```python
import functools

import jax
import jax.numpy as jnp
from jax import lax
from jax.experimental import pallas as pl
from jax.experimental.pallas import tpu as pltpu
from jax.sharding import PartitionSpec as P

ENERGY_LOW = -1.5
ENERGY_SPAN = 3.0
THERMAL = 0.1
LOSS_FLOOR = 0.05
LANES = 128
MARGIN = 0.02


def dot_exact(left_op, right_op):
    return jnp.dot(
        left_op,
        right_op,
        precision=lax.Precision.HIGHEST,
        preferred_element_type=jnp.float32,
    )


def stacked_dot(left_stack, right_op):
    return dot_exact(left_stack, right_op)


def combine(with_re, with_im):
    rows = with_re.shape[0] // 2
    return with_re[:rows] - with_im[rows:], with_re[rows:] + with_im[:rows]


def cmul(left_op, right_op):
    left_stack = jnp.concatenate(left_op, axis=0)
    return combine(stacked_dot(left_stack, right_op[0]), stacked_dot(left_stack, right_op[1]))


def split(value):
    high = value.astype(jnp.bfloat16)
    return high, (value - high.astype(jnp.float32)).astype(jnp.bfloat16)


def three_term(left_stack, right_op):
    left_hi, left_lo = left_stack
    right_hi, right_lo = right_op
    rows = left_hi.shape[0]
    wide = jnp.dot(
        jnp.concatenate([left_hi, left_lo], axis=0), right_hi, preferred_element_type=jnp.float32
    )
    narrow = jnp.dot(left_hi, right_lo, preferred_element_type=jnp.float32)
    return wide[:rows] + (wide[rows:] + narrow)


def cmul_split(left_stack, right_op):
    return combine(three_term(left_stack, right_op[0]), three_term(left_stack, right_op[1]))


def stack_split(value):
    return split(jnp.concatenate(value, axis=0))


def invert(matrix_re, matrix_im, x_ref):
    start = (jnp.transpose(matrix_re), -jnp.transpose(matrix_im))
    matrix_stack = stack_split((matrix_re, matrix_im))
    x_ref[0] = start[0]
    x_ref[1] = start[1]
    gram = cmul_split(matrix_stack, (split(start[0]), split(start[1])))
    sums = jnp.sum(jnp.abs(gram[0]) + jnp.abs(gram[1]), axis=0, keepdims=True)
    high = jnp.max(sums)
    low = jnp.float32(0.98 * LOSS_FLOOR * LOSS_FLOOR)

    def raised(low, scale):
        reach = scale * low
        return jnp.minimum(reach * (2.0 - reach), scale * (2.0 - scale))

    def step(x_re, x_im, product, scale, outer=1.0):
        x_stack = stack_split((x_re, x_im))
        next_re, next_im = cmul_split(x_stack, (split(product[0]), split(product[1])))
        x_ref[0] = (outer * scale) * (2.0 * x_re - scale * next_re)
        x_ref[1] = (outer * scale) * (2.0 * x_im - scale * next_im)

    low = low / high
    scale = 2.0 / (1.0 + jnp.maximum(low, MARGIN))
    step(start[0], start[1], tuple(part / high for part in gram), scale, 1.0 / high)
    low = raised(low, scale)

    def refine(low):
        x_re, x_im = x_ref[0], x_ref[1]
        product = cmul_split(matrix_stack, (split(x_re), split(x_im)))
        scale = 2.0 / (1.0 + jnp.maximum(low, MARGIN))
        step(x_re, x_im, product, scale)
        return raised(low, scale)

    low = lax.while_loop(lambda low: low < 0.998, refine, low)
    scale = 2.0 / (1.0 + low)
    x_re, x_im = x_ref[0], x_ref[1]
    product = cmul((matrix_re, matrix_im), (x_re, x_im))
    last_re, last_im = cmul((x_re, x_im), product)
    return scale * (2.0 * x_re - scale * last_re), scale * (2.0 * x_im - scale * last_im)


def take(ref, first):
    return ref[first], ref[first + 1]


def put(ref, first, value):
    ref[first] = value[0]
    ref[first + 1] = value[1]


def minus(left_op, right_op):
    return left_op[0] - right_op[0], left_op[1] - right_op[1]


def eliminate_kernel(carry, diag_a, diag_b, low_a, up_a, low_b, up_b, src_a, src_b,
                     first_out, second_out, reduced_out, x_ref):
    pivot = minus(take(diag_a, 0), cmul(take(low_a, 0), take(carry, 0)))
    source = minus(take(src_a, 0), cmul(take(low_a, 0), take(carry, 2)))
    inverse = invert(pivot[0], pivot[1], x_ref)
    put(first_out, 0, cmul(inverse, take(up_a, 0)))
    put(first_out, 2, cmul(inverse, source))
    pivot = minus(take(diag_b, 0), cmul(take(low_b, 0), take(first_out, 0)))
    source = minus(take(src_b, 0), cmul(take(low_b, 0), take(first_out, 2)))
    put(reduced_out, 0, pivot)
    put(reduced_out, 2, source)
    inverse = invert(pivot[0], pivot[1], x_ref)
    put(second_out, 0, cmul(inverse, take(up_b, 0)))
    put(second_out, 2, cmul(inverse, source))


def join_kernel(carry, reduced, up_b, value_out, x_ref):
    pivot = minus(take(reduced, 0), cmul(take(up_b, 0), take(carry, 0)))
    source = minus(take(reduced, 2), cmul(take(up_b, 0), take(carry, 2)))
    inverse = invert(pivot[0], pivot[1], x_ref)
    put(value_out, 0, cmul(inverse, source))


def back_kernel(value, second, first, second_out, first_out):
    result = minus(take(second, 2), cmul(take(second, 0), take(value, 0)))
    put(second_out, 0, result)
    put(first_out, 0, minus(take(first, 2), cmul(take(first, 0), result)))


def back_first_kernel(value, first, first_out):
    put(first_out, 0, minus(take(first, 2), cmul(take(first, 0), take(value, 0))))


def dot_rows(left_op, right_op):
    return lax.dot_general(
        left_op,
        right_op,
        (((1,), (1,)), ((), ())),
        precision=lax.Precision.HIGHEST,
        preferred_element_type=jnp.float32,
    )


def place(half, offset):
    row = lax.broadcasted_iota(jnp.int32, (half, half), 0)
    column = lax.broadcasted_iota(jnp.int32, (half, half), 1)
    return row, column


def pack(block_re, block_im):
    half = block_re.shape[0] // 2
    row, column = place(half, 0)
    top_re, top_im = block_re[:half, :half], block_im[:half, :half]
    low_re, low_im = block_re[half:, half:], block_im[half:, half:]
    both_re = jnp.where(column >= row, top_re, low_re)
    both_im = jnp.where(column > row, top_im, jnp.where(column == row, low_re, low_im))
    return (
        jnp.concatenate([both_re, block_re[:half, half:]], axis=1),
        jnp.concatenate([both_im, block_im[:half, half:]], axis=1),
    )


def unpack(packed_re, packed_im):
    half = packed_re.shape[0]
    row, column = place(half, 0)
    both_re, side_re = packed_re[:, :half], packed_re[:, half:]
    both_im, side_im = packed_im[:, :half], packed_im[:, half:]
    turned_re, turned_im = jnp.transpose(both_re), -jnp.transpose(both_im)
    top_re = jnp.where(column >= row, both_re, turned_re)
    low_re = jnp.where(column < row, both_re, jnp.where(column == row, both_im, turned_re))
    top_im = jnp.where(column > row, both_im, jnp.where(column == row, 0.0, turned_im))
    low_im = jnp.where(column < row, both_im, jnp.where(column == row, 0.0, turned_im))
    whole_re = jnp.concatenate(
        [
            jnp.concatenate([top_re, side_re], axis=1),
            jnp.concatenate([jnp.transpose(side_re), low_re], axis=1),
        ],
        axis=0,
    )
    whole_im = jnp.concatenate(
        [
            jnp.concatenate([top_im, side_im], axis=1),
            jnp.concatenate([-jnp.transpose(side_im), low_im], axis=1),
        ],
        axis=0,
    )
    return whole_re, whole_im


def fold(first, second):
    half = first.shape[0]
    return jnp.concatenate(
        [
            first[:, :LANES],
            second[:, :LANES],
            jnp.concatenate([first[:, LANES:], second[:, LANES:]], axis=1),
        ],
        axis=0,
    )


def unfold(rows_of, half):
    tail = rows_of[2 * half :]
    side = tail.shape[1] // 2
    return (
        jnp.concatenate([rows_of[:half], tail[:, :side]], axis=1),
        jnp.concatenate([rows_of[half : 2 * half], tail[:, side:]], axis=1),
    )


def exchange_kernel(count, half_way, value_a, value_b, weight, slot, polar_out,
                    packed, arrived, ordered, sums, returned, merged,
                    out_sem, in_sem, back_sem, home_sem):
    me = lax.axis_index("energy")
    left = lax.axis_index("transpor") < half_way
    order = value_a.shape[1]
    half = order // 2
    rows = sums.shape[2]
    barrier = pltpu.get_barrier_semaphore()
    for step in range(1, count):
        pl.semaphore_signal(
            barrier,
            inc=1,
            device_id={"energy": lax.rem(me + step, count)},
            device_id_type=pl.DeviceIdType.MESH,
        )
    kinds = [[], []]
    for first, second in ((value_a, value_b), (value_b, value_a)):
        state_re = jnp.where(left, first[0], second[0])
        state_im = jnp.where(left, first[1], second[1])
        for kind in range(2):
            held = weight[kind : kind + 1, :]
            stack = jnp.concatenate([state_re * held, state_im * held], axis=0)
            with_re = dot_rows(stack, state_re)
            with_im = dot_rows(stack, state_im)
            kinds[kind].append(
                pack(with_re[:order] + with_im[order:], with_re[order:] - with_im[:order])
            )
    for kind in range(2):
        for part in range(2):
            flat = fold(kinds[kind][0][part], kinds[kind][1][part])
            for piece in range(count):
                packed[piece, 2 * kind + part, :rows] = flat[piece * rows : (piece + 1) * rows]
    for piece in range(count):
        for part in range(4):
            packed[piece, part, rows:] = slot[...]
    pl.semaphore_wait(barrier, count - 1)

    def there(step):
        other = lax.rem(me + step, count)
        return pltpu.make_async_remote_copy(
            src_ref=packed.at[other],
            dst_ref=arrived.at[me],
            send_sem=out_sem.at[step],
            recv_sem=in_sem.at[step],
            device_id={"energy": other},
            device_id_type=pl.DeviceIdType.MESH,
        )

    for step in range(1, count):
        there(step).start()
    arrived[me] = packed[me]
    for step in range(1, count):
        there(step).wait_recv()

    own = me * rows + lax.broadcasted_iota(jnp.int32, (rows, LANES), 0)
    lane = lax.broadcasted_iota(jnp.int32, (rows, LANES), 1)
    within = jnp.where(own >= half, own - half, own)
    on_diagonal = (own < order) & (lane == within)
    for position in range(count):
        total = [jnp.zeros((rows, LANES), jnp.float32)] * 4
        for source in range(count):
            here = arrived[source, 0, rows:] == position
            total = [
                jnp.where(here, arrived[source, part, :rows], total[part]) for part in range(4)
            ]
        ordered[position, 0] = total[0]
        ordered[position, 1] = total[1]
        ordered[position, 2] = total[2]
        ordered[position, 3] = jnp.where(on_diagonal, 0.0, total[3])
        ordered[position, 4] = jnp.where(on_diagonal, total[3], total[2])
    for lag in range(count):
        sum_re = jnp.zeros((rows, LANES), jnp.float32)
        sum_im = jnp.zeros((rows, LANES), jnp.float32)
        for position in range(lag, count):
            before = position - lag
            lesser_re, lesser_im = ordered[position, 0], ordered[position, 1]
            greater_im = ordered[before, 3]
            sum_re = sum_re + (lesser_re * ordered[before, 2] + lesser_im * greater_im)
            sum_im = sum_im + (lesser_im * ordered[before, 4] - lesser_re * greater_im)
        sums[lag, 0] = sum_re / count
        sums[lag, 1] = sum_im / count

    def back(step):
        other = lax.rem(me + step, count)
        return pltpu.make_async_remote_copy(
            src_ref=sums.at[other],
            dst_ref=returned.at[me],
            send_sem=back_sem.at[step],
            recv_sem=home_sem.at[step],
            device_id={"energy": other},
            device_id_type=pl.DeviceIdType.MESH,
        )

    for step in range(1, count):
        back(step).start()
    returned[me] = sums[me]
    for step in range(1, count):
        back(step).wait_recv()
    for piece in range(count):
        for part in range(2):
            merged[part, piece * rows : (piece + 1) * rows] = returned[piece, part]
    parts = [unfold(merged[part], half) for part in range(2)]
    for block in range(2):
        whole_re, whole_im = unpack(parts[0][block], parts[1][block])
        polar_out[0, block, 0] = whole_re
        polar_out[0, block, 1] = whole_im
    for step in range(1, count):
        there(step).wait_send()
        back(step).wait_send()


def exchange(value_a, value_b, weight, slot, count, half_way):
    order = value_a.shape[1]
    rows = order * order // LANES // count
    dma = pltpu.SemaphoreType.DMA((count,))
    return pl.pallas_call(
        functools.partial(exchange_kernel, count, half_way),
        out_shape=jax.ShapeDtypeStruct((1, 2, 2, order, order), jnp.float32),
        scratch_shapes=[
            pltpu.VMEM((count, 4, rows + 1, LANES), jnp.float32),
            pltpu.VMEM((count, 4, rows + 1, LANES), jnp.float32),
            pltpu.VMEM((count, 5, rows, LANES), jnp.float32),
            pltpu.VMEM((count, 2, rows, LANES), jnp.float32),
            pltpu.VMEM((count, 2, rows, LANES), jnp.float32),
            pltpu.VMEM((2, rows * count, LANES), jnp.float32),
            dma,
            dma,
            dma,
            dma,
        ],
        compiler_params=pltpu.CompilerParams(
            collective_id=0, has_side_effects=True, vmem_limit_bytes=48 * 1024 * 1024
        ),
    )(value_a, value_b, weight, slot)


def call(body, counts, order, scratch=True):
    shapes = [jax.ShapeDtypeStruct((count, order, order), jnp.float32) for count in counts]
    return pl.pallas_call(
        body,
        out_shape=shapes,
        scratch_shapes=[pltpu.VMEM((2, order, order), jnp.float32)] if scratch else [],
        compiler_params=pltpu.CompilerParams(vmem_limit_bytes=48 * 1024 * 1024),
    )


def passed_along(x, axis, by):
    length = lax.axis_size(axis)
    pairs = [(i, i + by) for i in range(length) if 0 <= i + by < length]
    return lax.ppermute(x, axis, pairs)


def product_hi(left_op, right_op):
    return jnp.einsum("...ik,...kj->...ij", left_op, right_op, precision=lax.Precision.HIGHEST)


def complex_mul(left_op, right_op):
    left_re, left_im = (left_op[..., 0, :, :], left_op[..., 1, :, :])
    right_re, right_im = (right_op[..., 0, :, :], right_op[..., 1, :, :])
    real_part = product_hi(left_re, right_re) - product_hi(left_im, right_im)
    imag_part = product_hi(left_re, right_im) + product_hi(left_im, right_re)
    return jnp.stack([real_part, imag_part], axis=-3)


def complex_adj(matrix):
    return jnp.stack(
        [jnp.swapaxes(matrix[..., 0, :, :], -1, -2), -jnp.swapaxes(matrix[..., 1, :, :], -1, -2)],
        axis=-3,
    )


def per_device(ham_diag, ham_hop, inject, chemical, energy_slot, onsite_shift, onsite_loss):
    orbitals = ham_diag.shape[2]
    energies = energy_slot.shape[0]
    partitions = lax.axis_size("transpor")
    half = partitions // 2
    my_index = lax.axis_index("transpor")
    grid_total = energies * lax.axis_size("energy")
    high = lax.Precision.HIGHEST
    energy = ENERGY_LOW + ENERGY_SPAN * (energy_slot.astype(jnp.float32) + 0.5) / grid_total
    identity = jnp.eye(orbitals, dtype=jnp.float32)
    real_part = (
        energy[0] * identity - ham_diag[:, 0] - onsite_shift[0, :, :, None] * identity
    )
    imag_part = -ham_diag[:, 1] + onsite_loss[0, :, :, None] * identity
    contact = complex_mul(ham_hop[-1], complex_adj(ham_hop[-1]))
    is_last = (my_index == partitions - 1).astype(jnp.float32)
    real_part = real_part.at[-1].add(-is_last * contact[1])
    imag_part = imag_part.at[-1].add(is_last * contact[0])
    diag_blocks = jnp.stack([real_part, imag_part], axis=1)
    prev_hop = passed_along(ham_hop[-1], "transpor", 1)
    from_left = my_index < half

    def pick(left_op, right_op):
        return jnp.where(from_left, left_op, right_op)

    diag_a = pick(diag_blocks[0], diag_blocks[1])
    diag_b = pick(diag_blocks[1], diag_blocks[0])
    src_a = pick(inject[0], inject[1])
    src_b = pick(inject[1], inject[0])
    behind = -complex_adj(prev_hop)
    within = -complex_adj(ham_hop[0])
    low_a = pick(behind, -ham_hop[1])
    up_a = pick(-ham_hop[0], within)
    low_b = pick(within, -ham_hop[0])
    up_b = pick(-ham_hop[1], behind)

    carry = jnp.zeros((4, orbitals, orbitals), jnp.float32)
    kept = (carry, carry, carry)
    eliminate = call(eliminate_kernel, (4, 4, 4), orbitals)
    for stage in range(half):
        active = (my_index == stage) | (my_index == partitions - 1 - stage)
        kept = lax.cond(
            active,
            lambda now, then: tuple(
                eliminate(now, diag_a, diag_b, low_a, up_a, low_b, up_b, src_a, src_b)
            ),
            lambda now, then: then,
            carry,
            kept,
        )
        other = partitions - 1 - stage
        if stage < half - 1:
            pairs = [(stage, stage + 1), (other, other - 1)]
        else:
            pairs = [(stage, other), (other, stage)]
        carry = lax.ppermute(kept[1], "transpor", pairs)
    first, second, reduced = kept
    middle = (my_index == half - 1) | (my_index == half)
    (value_b,) = call(join_kernel, (2,), orbitals)(carry, reduced, up_b)
    (value_a,) = call(back_first_kernel, (2,), orbitals, False)(value_b, first)
    for stage in range(half - 2, -1, -1):
        other = partitions - 1 - stage
        passed = lax.ppermute(value_a, "transpor", [(stage + 1, stage), (other - 1, other)])
        new_b, new_a = call(back_kernel, (2, 2), orbitals, False)(passed, second, first)
        active = (my_index == stage) | (my_index == other)
        value_b = jnp.where(active, new_b, value_b)
        value_a = jnp.where(active, new_a, value_a)
    occupied = 1.0 / (1.0 + jnp.exp((energy[0] - chemical[None, :]) / THERMAL))
    weight = jnp.concatenate([occupied, 1.0 - occupied], axis=0)
    slot = jnp.full((1, LANES), energy_slot[0].astype(jnp.float32))
    return exchange(value_a, value_b, weight, slot, grid_total, half)


def solution(mesh):
    in_specs = (
        P("transpor", None, None, None),
        P("transpor", None, None, None),
        P("transpor", None, None, None),
        P(),
        P("energy"),
        P("energy", "transpor", None),
        P("energy", "transpor", None),
    )
    out_specs = P("energy", "transpor", None, None, None)
    return jax.shard_map(
        per_device, mesh=mesh, in_specs=in_specs, out_specs=out_specs, check_vma=False
    )
```

```python
import functools

import jax
import jax.numpy as jnp
from jax import lax
from jax.experimental import pallas as pl
from jax.experimental.pallas import tpu as pltpu
from jax.sharding import PartitionSpec as P

ENERGY_LOW = -1.5
ENERGY_SPAN = 3.0
THERMAL = 0.1
LOSS_FLOOR = 0.05
LANES = 128
MARGIN = 0.02


def one_term(left_op, right_op):
    return jnp.dot(left_op, right_op, preferred_element_type=jnp.float32)


def one_term_rows(left_op, right_op):
    dims = (((1,), (1,)), ((), ()))
    return lax.dot_general(left_op, right_op, dims, preferred_element_type=jnp.float32)


def split(value, count=2):
    parts = []
    for part in range(count):
        parts.append(value.astype(jnp.bfloat16))
        if part < count - 1:
            value = value - parts[-1].astype(jnp.float32)
    return parts


def multiply(left_op, right_op, dot=one_term):
    count = len(left_op)
    total = None
    for place in range(count - 1, -1, -1):
        for first in range(place + 1):
            term = dot(left_op[first], right_op[place - first])
            total = term if total is None else total + term
    return total


def ready(value, count=2):
    return tuple(split(part, count) for part in (value[0], value[1], value[0] + value[1]))


def cmul_ready(left_op, right_op):
    first = multiply(left_op[0], right_op[0])
    second = multiply(left_op[1], right_op[1])
    third = multiply(left_op[2], right_op[2])
    return first - second, third - first - second


def ready_turned(value):
    return tuple(split(part) for part in (value[0], value[1], value[0] - value[1]))


def cmul_turned(left_op, right_op):
    first = multiply(left_op[0], right_op[0], one_term_rows)
    second = multiply(left_op[1], right_op[1], one_term_rows)
    third = multiply(left_op[2], right_op[2], one_term_rows)
    return first + second, third - first + second


def adjoint(value):
    return jnp.transpose(value[0]), -jnp.transpose(value[1])


def on_diagonal_of(order):
    row = lax.broadcasted_iota(jnp.int32, (order, order), 0)
    column = lax.broadcasted_iota(jnp.int32, (order, order), 1)
    return row == column


def invert(matrix, x_ref):
    start = adjoint(matrix)
    matrix_ready = ready(matrix)
    gram = cmul_ready(matrix_ready, ready(start))
    high = jnp.max(jnp.sum(jnp.abs(gram[0]) + jnp.abs(gram[1]), axis=0, keepdims=True))
    inner = 1.0 / high

    def raised(low, scale):
        reach = scale * low
        return jnp.minimum(reach * (2.0 - reach), scale * (2.0 - scale))

    def scale_for(low):
        return 2.0 / (1.0 + jnp.maximum(low, MARGIN))

    def step(x, x_ready, product, scale, outer):
        change = cmul_ready(x_ready, ready(product))
        x_ref[0] = outer * (2.0 * x[0] - scale * change[0])
        x_ref[1] = outer * (2.0 * x[1] - scale * change[1])

    low = jnp.float32(0.98 * LOSS_FLOOR * LOSS_FLOOR) * inner
    scale = scale_for(low)
    step(start, ready(start), gram, scale * inner, scale * inner)
    low = raised(low, scale)

    def refine(low):
        x = (x_ref[0], x_ref[1])
        x_ready = ready(x)
        product = cmul_ready(matrix_ready, x_ready)
        scale = scale_for(low)
        step(x, x_ready, product, scale, scale)
        return raised(low, scale)

    low = lax.while_loop(lambda low: low < 0.998, refine, low)
    scale = 2.0 / (1.0 + low)
    x = (x_ref[0], x_ref[1])
    product = cmul_ready(ready(matrix, 3), ready(x, 3))
    aim = jnp.where(on_diagonal_of(matrix[0].shape[0]), 2.0 * scale - 1.0, 0.0)
    left_over = (aim - scale * scale * product[0], -(scale * scale) * product[1])
    change = cmul_ready(ready(x), ready(left_over))
    return x[0] + change[0], x[1] + change[1]


def take(ref, first):
    return ref[first], ref[first + 1]


def put(ref, first, value):
    ref[first] = value[0]
    ref[first + 1] = value[1]


def minus(left_op, right_op):
    return left_op[0] - right_op[0], left_op[1] - right_op[1]


def negated(value):
    return -value[0], -value[1]


def pick(left, first, second):
    return jnp.where(left, first[0], second[0]), jnp.where(left, first[1], second[1])


def couplings(left, hop, prev):
    behind = negated(adjoint((prev[0], prev[1])))
    within = negated(adjoint((hop[0, 0], hop[0, 1])))
    inner = negated((hop[0, 0], hop[0, 1]))
    onward = negated((hop[1, 0], hop[1, 1]))
    return (
        lambda: pick(left, behind, onward),
        lambda: pick(left, inner, within),
        lambda: pick(left, within, inner),
        lambda: pick(left, onward, behind),
    )


def eliminate_kernel(starts, partitions, carry, diag, hop, prev, inject, shift, loss, energy,
                     first_out, second_out, reduced_out, x_ref):
    my_index = lax.axis_index("transpor")
    left = my_index < partitions // 2
    is_last = jnp.where(my_index == partitions - 1, 1.0, 0.0)
    where_diag = on_diagonal_of(diag.shape[2])
    contact_op = (hop[1, 0], hop[1, 1])
    contact = cmul_turned(ready(contact_op), ready_turned(contact_op))
    blocks = []
    for block in range(2):
        level = energy[...] - shift[block : block + 1]
        block_re = jnp.where(where_diag, level, 0.0) - diag[block, 0]
        block_im = jnp.where(where_diag, loss[block : block + 1], 0.0) - diag[block, 1]
        if block == 1:
            block_re = block_re - is_last * contact[1]
            block_im = block_im + is_last * contact[0]
        blocks.append((block_re, block_im))
    low_a, up_a, low_b, up_b = couplings(left, hop, prev)
    sources = [(inject[block, 0], inject[block, 1]) for block in range(2)]

    pivot = pick(left, blocks[0], blocks[1])
    source = pick(left, sources[0], sources[1])
    if not starts:
        back = ready(low_a())
        pivot = minus(pivot, cmul_ready(back, ready(take(carry, 0))))
        source = minus(source, cmul_ready(back, ready(take(carry, 2))))
    put(reduced_out, 0, pick(left, blocks[1], blocks[0]))
    inverse = ready(invert(pivot, x_ref))
    on = cmul_ready(inverse, ready(up_a()))
    put(first_out, 0, on)
    held = cmul_ready(inverse, ready(source))
    put(first_out, 2, held)
    back = ready(low_b())
    pivot = minus(take(reduced_out, 0), cmul_ready(back, ready(on)))
    source = minus(pick(left, sources[1], sources[0]), cmul_ready(back, ready(held)))
    put(reduced_out, 0, pivot)
    put(reduced_out, 2, source)
    inverse = ready(invert(pivot, x_ref))
    put(second_out, 0, cmul_ready(inverse, ready(up_b())))
    put(second_out, 2, cmul_ready(inverse, ready(source)))


def join_kernel(partitions, carry, reduced, first, hop, prev, value_out, first_value_out, x_ref):
    left = lax.axis_index("transpor") < partitions // 2
    on = ready(couplings(left, hop, prev)[3]())
    pivot = minus(take(reduced, 0), cmul_ready(on, ready(take(carry, 0))))
    source = minus(take(reduced, 2), cmul_ready(on, ready(take(carry, 2))))
    inverse = ready(invert(pivot, x_ref))
    value = cmul_ready(inverse, ready(source))
    put(value_out, 0, value)
    change = cmul_ready(ready(take(first, 0)), ready(value))
    put(first_value_out, 0, minus(take(first, 2), change))


def back_kernel(value, second, first, second_out, first_out):
    change = cmul_ready(ready(take(second, 0)), ready(take(value, 0)))
    result = minus(take(second, 2), change)
    put(second_out, 0, result)
    change = cmul_ready(ready(take(first, 0)), ready(result))
    put(first_out, 0, minus(take(first, 2), change))


def place(half, offset):
    row = lax.broadcasted_iota(jnp.int32, (half, half), 0)
    column = lax.broadcasted_iota(jnp.int32, (half, half), 1)
    return row, column


def pack(block_re, block_im):
    half = block_re.shape[0] // 2
    row, column = place(half, 0)
    top_re, top_im = block_re[:half, :half], block_im[:half, :half]
    low_re, low_im = block_re[half:, half:], block_im[half:, half:]
    both_re = jnp.where(column >= row, top_re, low_re)
    both_im = jnp.where(column > row, top_im, jnp.where(column == row, low_re, low_im))
    return (
        jnp.concatenate([both_re, block_re[:half, half:]], axis=1),
        jnp.concatenate([both_im, block_im[:half, half:]], axis=1),
    )


def unpack(packed_re, packed_im):
    half = packed_re.shape[0]
    row, column = place(half, 0)
    both_re, side_re = packed_re[:, :half], packed_re[:, half:]
    both_im, side_im = packed_im[:, :half], packed_im[:, half:]
    turned_re, turned_im = jnp.transpose(both_re), -jnp.transpose(both_im)
    top_re = jnp.where(column >= row, both_re, turned_re)
    low_re = jnp.where(column < row, both_re, jnp.where(column == row, both_im, turned_re))
    top_im = jnp.where(column > row, both_im, jnp.where(column == row, 0.0, turned_im))
    low_im = jnp.where(column < row, both_im, jnp.where(column == row, 0.0, turned_im))
    whole_re = jnp.concatenate(
        [
            jnp.concatenate([top_re, side_re], axis=1),
            jnp.concatenate([jnp.transpose(side_re), low_re], axis=1),
        ],
        axis=0,
    )
    whole_im = jnp.concatenate(
        [
            jnp.concatenate([top_im, side_im], axis=1),
            jnp.concatenate([-jnp.transpose(side_im), low_im], axis=1),
        ],
        axis=0,
    )
    return whole_re, whole_im


def fold(first, second):
    half = first.shape[0]
    return jnp.concatenate(
        [
            first[:, :LANES],
            second[:, :LANES],
            jnp.concatenate([first[:, LANES:], second[:, LANES:]], axis=1),
        ],
        axis=0,
    )


def unfold(rows_of, half):
    tail = rows_of[2 * half :]
    side = tail.shape[1] // 2
    return (
        jnp.concatenate([rows_of[:half], tail[:, :side]], axis=1),
        jnp.concatenate([rows_of[half : 2 * half], tail[:, side:]], axis=1),
    )


def exchange_kernel(count, half_way, value_a, value_b, weight, slot, polar_out,
                    packed, arrived, ordered, sums, returned, merged,
                    out_sem, in_sem, back_sem, home_sem):
    me = lax.axis_index("energy")
    left = lax.axis_index("transpor") < half_way
    order = value_a.shape[1]
    half = order // 2
    rows = sums.shape[2]
    barrier = pltpu.get_barrier_semaphore()
    for step in range(1, count):
        pl.semaphore_signal(
            barrier,
            inc=1,
            device_id={"energy": lax.rem(me + step, count)},
            device_id_type=pl.DeviceIdType.MESH,
        )
    kinds = [[], []]
    for first, second in ((value_a, value_b), (value_b, value_a)):
        state_re = jnp.where(left, first[0], second[0])
        state_im = jnp.where(left, first[1], second[1])
        turned = ready_turned((state_re, state_im))
        for kind in range(2):
            held = weight[kind : kind + 1, :]
            weighted = ready((state_re * held, state_im * held))
            kinds[kind].append(pack(*cmul_turned(weighted, turned)))
    for kind in range(2):
        for part in range(2):
            flat = fold(kinds[kind][0][part], kinds[kind][1][part])
            for piece in range(count):
                packed[piece, 2 * kind + part, :rows] = flat[piece * rows : (piece + 1) * rows]
    for piece in range(count):
        for part in range(4):
            packed[piece, part, rows:] = slot[...]
    pl.semaphore_wait(barrier, count - 1)

    def there(step):
        other = lax.rem(me + step, count)
        return pltpu.make_async_remote_copy(
            src_ref=packed.at[other],
            dst_ref=arrived.at[me],
            send_sem=out_sem.at[step],
            recv_sem=in_sem.at[step],
            device_id={"energy": other},
            device_id_type=pl.DeviceIdType.MESH,
        )

    for step in range(1, count):
        there(step).start()
    arrived[me] = packed[me]
    for step in range(1, count):
        there(step).wait_recv()

    own = me * rows + lax.broadcasted_iota(jnp.int32, (rows, LANES), 0)
    lane = lax.broadcasted_iota(jnp.int32, (rows, LANES), 1)
    within = jnp.where(own >= half, own - half, own)
    on_diagonal = (own < order) & (lane == within)
    for position in range(count):
        total = [jnp.zeros((rows, LANES), jnp.float32)] * 4
        for source in range(count):
            here = arrived[source, 0, rows:] == position
            total = [
                jnp.where(here, arrived[source, part, :rows], total[part]) for part in range(4)
            ]
        ordered[position, 0] = total[0]
        ordered[position, 1] = total[1]
        ordered[position, 2] = total[2]
        ordered[position, 3] = jnp.where(on_diagonal, 0.0, total[3])
        ordered[position, 4] = jnp.where(on_diagonal, total[3], total[2])
    for lag in range(count):
        sum_re = jnp.zeros((rows, LANES), jnp.float32)
        sum_im = jnp.zeros((rows, LANES), jnp.float32)
        for position in range(lag, count):
            before = position - lag
            lesser_re, lesser_im = ordered[position, 0], ordered[position, 1]
            greater_im = ordered[before, 3]
            sum_re = sum_re + (lesser_re * ordered[before, 2] + lesser_im * greater_im)
            sum_im = sum_im + (lesser_im * ordered[before, 4] - lesser_re * greater_im)
        sums[lag, 0] = sum_re / count
        sums[lag, 1] = sum_im / count

    def back(step):
        other = lax.rem(me + step, count)
        return pltpu.make_async_remote_copy(
            src_ref=sums.at[other],
            dst_ref=returned.at[me],
            send_sem=back_sem.at[step],
            recv_sem=home_sem.at[step],
            device_id={"energy": other},
            device_id_type=pl.DeviceIdType.MESH,
        )

    for step in range(1, count):
        back(step).start()
    returned[me] = sums[me]
    for step in range(1, count):
        back(step).wait_recv()
    for piece in range(count):
        for part in range(2):
            merged[part, piece * rows : (piece + 1) * rows] = returned[piece, part]
    parts = [unfold(merged[part], half) for part in range(2)]
    for block in range(2):
        whole_re, whole_im = unpack(parts[0][block], parts[1][block])
        polar_out[0, block, 0] = whole_re
        polar_out[0, block, 1] = whole_im
    for step in range(1, count):
        there(step).wait_send()
        back(step).wait_send()


def exchange(value_a, value_b, weight, slot, count, half_way):
    order = value_a.shape[1]
    rows = order * order // LANES // count
    dma = pltpu.SemaphoreType.DMA((count,))
    return pl.pallas_call(
        functools.partial(exchange_kernel, count, half_way),
        out_shape=jax.ShapeDtypeStruct((1, 2, 2, order, order), jnp.float32),
        scratch_shapes=[
            pltpu.VMEM((count, 4, rows + 1, LANES), jnp.float32),
            pltpu.VMEM((count, 4, rows + 1, LANES), jnp.float32),
            pltpu.VMEM((count, 5, rows, LANES), jnp.float32),
            pltpu.VMEM((count, 2, rows, LANES), jnp.float32),
            pltpu.VMEM((count, 2, rows, LANES), jnp.float32),
            pltpu.VMEM((2, rows * count, LANES), jnp.float32),
            dma,
            dma,
            dma,
            dma,
        ],
        compiler_params=pltpu.CompilerParams(
            collective_id=0, has_side_effects=True, vmem_limit_bytes=48 * 1024 * 1024
        ),
    )(value_a, value_b, weight, slot)


def call(body, counts, order, scratch=True):
    shapes = [jax.ShapeDtypeStruct((count, order, order), jnp.float32) for count in counts]
    return pl.pallas_call(
        body,
        out_shape=shapes,
        scratch_shapes=[pltpu.VMEM((2, order, order), jnp.float32)] if scratch else [],
        compiler_params=pltpu.CompilerParams(vmem_limit_bytes=48 * 1024 * 1024),
    )


def passed_along(x, axis, by):
    length = lax.axis_size(axis)
    pairs = [(i, i + by) for i in range(length) if 0 <= i + by < length]
    return lax.ppermute(x, axis, pairs)


def per_device(ham_diag, ham_hop, inject, chemical, energy_slot, onsite_shift, onsite_loss):
    orbitals = ham_diag.shape[2]
    energies = energy_slot.shape[0]
    partitions = lax.axis_size("transpor")
    half = partitions // 2
    my_index = lax.axis_index("transpor")
    grid_total = energies * lax.axis_size("energy")
    energy = ENERGY_LOW + ENERGY_SPAN * (energy_slot.astype(jnp.float32) + 0.5) / grid_total
    prev_hop = passed_along(ham_hop[-1], "transpor", 1)
    levels = jnp.full((1, orbitals), energy[0])
    shift, loss = onsite_shift[0], onsite_loss[0]

    carry = jnp.zeros((4, orbitals, orbitals), jnp.float32)
    kept = (carry, carry, carry)
    for stage in range(half):
        active = (my_index == stage) | (my_index == partitions - 1 - stage)
        body = functools.partial(eliminate_kernel, stage == 0, partitions)
        eliminate = call(body, (4, 4, 4), orbitals)
        kept = lax.cond(
            active,
            lambda now, then, eliminate=eliminate: tuple(
                eliminate(now, ham_diag, ham_hop, prev_hop, inject, shift, loss, levels)
            ),
            lambda now, then: then,
            carry,
            kept,
        )
        other = partitions - 1 - stage
        if stage < half - 1:
            pairs = [(stage, stage + 1), (other, other - 1)]
        else:
            pairs = [(stage, other), (other, stage)]
        carry = lax.ppermute(kept[1], "transpor", pairs)
    first, second, reduced = kept
    join = call(functools.partial(join_kernel, partitions), (2, 2), orbitals)
    value_b, value_a = join(carry, reduced, first, ham_hop, prev_hop)
    for stage in range(half - 2, -1, -1):
        other = partitions - 1 - stage
        passed = lax.ppermute(value_a, "transpor", [(stage + 1, stage), (other - 1, other)])
        new_b, new_a = call(back_kernel, (2, 2), orbitals, False)(passed, second, first)
        active = (my_index == stage) | (my_index == other)
        value_b = jnp.where(active, new_b, value_b)
        value_a = jnp.where(active, new_a, value_a)
    occupied = 1.0 / (1.0 + jnp.exp((energy[0] - chemical[None, :]) / THERMAL))
    weight = jnp.concatenate([occupied, 1.0 - occupied], axis=0)
    slot = jnp.full((1, LANES), energy_slot[0].astype(jnp.float32))
    return exchange(value_a, value_b, weight, slot, grid_total, half)


def solution(mesh):
    in_specs = (
        P("transpor", None, None, None),
        P("transpor", None, None, None),
        P("transpor", None, None, None),
        P(),
        P("energy"),
        P("energy", "transpor", None),
        P("energy", "transpor", None),
    )
    out_specs = P("energy", "transpor", None, None, None)
    return jax.shard_map(
        per_device, mesh=mesh, in_specs=in_specs, out_specs=out_specs, check_vma=False
    )
```

```python
import functools

import jax
import jax.numpy as jnp
from jax import lax
from jax.experimental import pallas as pl
from jax.experimental.pallas import tpu as pltpu
from jax.sharding import PartitionSpec as P

ENERGY_LOW = -1.5
ENERGY_SPAN = 3.0
THERMAL = 0.1
LOSS_FLOOR = 0.05
LANES = 128
MARGIN = 0.02


def one_term(left_op, right_op):
    return jnp.dot(left_op, right_op, preferred_element_type=jnp.float32)


def one_term_rows(left_op, right_op):
    dims = (((1,), (1,)), ((), ()))
    return lax.dot_general(left_op, right_op, dims, preferred_element_type=jnp.float32)


def split(value, count=2):
    parts = []
    for part in range(count):
        parts.append(value.astype(jnp.bfloat16))
        if part < count - 1:
            value = value - parts[-1].astype(jnp.float32)
    return parts


def multiply(left_op, right_op, dot=one_term):
    count = len(left_op)
    total = None
    for place in range(count - 1, -1, -1):
        for first in range(place + 1):
            term = dot(left_op[first], right_op[place - first])
            total = term if total is None else total + term
    return total


def ready(value, count=2):
    return tuple(split(part, count) for part in (value[0], value[1], value[0] + value[1]))


def cmul_ready(left_op, right_op):
    first = multiply(left_op[0], right_op[0])
    second = multiply(left_op[1], right_op[1])
    third = multiply(left_op[2], right_op[2])
    return first - second, third - first - second


def ready_turned(value):
    return tuple(split(part) for part in (value[0], value[1], value[0] - value[1]))


def cmul_turned(left_op, right_op):
    first = multiply(left_op[0], right_op[0], one_term_rows)
    second = multiply(left_op[1], right_op[1], one_term_rows)
    third = multiply(left_op[2], right_op[2], one_term_rows)
    return first + second, third - first + second


def adjoint(value):
    return jnp.transpose(value[0]), -jnp.transpose(value[1])


def on_diagonal_of(order):
    row = lax.broadcasted_iota(jnp.int32, (order, order), 0)
    column = lax.broadcasted_iota(jnp.int32, (order, order), 1)
    return row == column


def invert(matrix, x_ref):
    start = adjoint(matrix)
    matrix_ready = ready(matrix)
    gram = cmul_ready(matrix_ready, ready(start))
    high = jnp.max(jnp.sum(jnp.abs(gram[0]) + jnp.abs(gram[1]), axis=0, keepdims=True))
    inner = 1.0 / high

    def raised(low, scale):
        reach = scale * low
        return jnp.minimum(reach * (2.0 - reach), scale * (2.0 - scale))

    def scale_for(low):
        return 2.0 / (1.0 + jnp.maximum(low, MARGIN))

    def step(x, x_ready, product, scale, outer):
        change = cmul_ready(x_ready, ready(product))
        x_ref[0] = outer * (2.0 * x[0] - scale * change[0])
        x_ref[1] = outer * (2.0 * x[1] - scale * change[1])

    low = jnp.float32(0.98 * LOSS_FLOOR * LOSS_FLOOR) * inner
    scale = scale_for(low)
    step(start, ready(start), gram, scale * inner, scale * inner)
    low = raised(low, scale)

    def refine(low):
        x = (x_ref[0], x_ref[1])
        x_ready = ready(x)
        product = cmul_ready(matrix_ready, x_ready)
        scale = scale_for(low)
        step(x, x_ready, product, scale, scale)
        return raised(low, scale)

    low = lax.while_loop(lambda low: low < 0.998, refine, low)
    scale = 2.0 / (1.0 + low)
    x = (x_ref[0], x_ref[1])
    product = cmul_ready(ready(matrix, 3), ready(x, 3))
    aim = jnp.where(on_diagonal_of(matrix[0].shape[0]), 2.0 * scale - 1.0, 0.0)
    left_over = (aim - scale * scale * product[0], -(scale * scale) * product[1])
    change = cmul_ready(ready(x), ready(left_over))
    return x[0] + change[0], x[1] + change[1]


def take(ref, first):
    return ref[first], ref[first + 1]


def put(ref, first, value):
    ref[first] = value[0]
    ref[first + 1] = value[1]


def minus(left_op, right_op):
    return left_op[0] - right_op[0], left_op[1] - right_op[1]


def negated(value):
    return -value[0], -value[1]


def pick(left, first, second):
    return jnp.where(left, first[0], second[0]), jnp.where(left, first[1], second[1])


def couplings(left, hop, prev):
    behind = negated(adjoint((prev[0], prev[1])))
    within = negated(adjoint((hop[0, 0], hop[0, 1])))
    inner = negated((hop[0, 0], hop[0, 1]))
    onward = negated((hop[1, 0], hop[1, 1]))
    return (
        lambda: pick(left, behind, onward),
        lambda: pick(left, inner, within),
        lambda: pick(left, within, inner),
        lambda: pick(left, onward, behind),
    )


def eliminate_kernel(starts, partitions, carry_on, carry_held, diag, hop, prev, inject, shift,
                     loss, energy, first_out, on_out, held_out, reduced_out, x_ref):
    my_index = lax.axis_index("transpor")
    left = my_index < partitions // 2
    is_last = jnp.where(my_index == partitions - 1, 1.0, 0.0)
    where_diag = on_diagonal_of(diag.shape[2])
    contact_op = (hop[1, 0], hop[1, 1])
    contact = cmul_turned(ready(contact_op), ready_turned(contact_op))
    blocks = []
    for block in range(2):
        level = energy[...] - shift[block : block + 1]
        block_re = jnp.where(where_diag, level, 0.0) - diag[block, 0]
        block_im = jnp.where(where_diag, loss[block : block + 1], 0.0) - diag[block, 1]
        if block == 1:
            block_re = block_re - is_last * contact[1]
            block_im = block_im + is_last * contact[0]
        blocks.append((block_re, block_im))
    low_a, up_a, low_b, up_b = couplings(left, hop, prev)
    sources = [(inject[block, 0], inject[block, 1]) for block in range(2)]

    pivot = pick(left, blocks[0], blocks[1])
    source = pick(left, sources[0], sources[1])
    if not starts:
        back = ready(low_a())
        pivot = minus(pivot, cmul_ready(back, ready(take(carry_on, 0))))
        source = minus(source, cmul_ready(back, ready(take(carry_held, 0))))
    put(reduced_out, 0, pick(left, blocks[1], blocks[0]))
    inverse = ready(invert(pivot, x_ref))
    on = cmul_ready(inverse, ready(up_a()))
    put(first_out, 0, on)
    held = cmul_ready(inverse, ready(source))
    put(first_out, 2, held)
    back = ready(low_b())
    pivot = minus(take(reduced_out, 0), cmul_ready(back, ready(on)))
    source = minus(pick(left, sources[1], sources[0]), cmul_ready(back, ready(held)))
    put(reduced_out, 0, pivot)
    put(reduced_out, 2, source)
    inverse = ready(invert(pivot, x_ref))
    put(on_out, 0, cmul_ready(inverse, ready(up_b())))
    put(held_out, 0, cmul_ready(inverse, ready(source)))


def join_inverse_kernel(partitions, carry_on, reduced, hop, prev, inverse_out, x_ref):
    left = lax.axis_index("transpor") < partitions // 2
    on = ready(couplings(left, hop, prev)[3]())
    pivot = minus(take(reduced, 0), cmul_ready(on, ready(take(carry_on, 0))))
    put(inverse_out, 0, invert(pivot, x_ref))


def join_value_kernel(partitions, carry_held, inverse, reduced, first, hop, prev,
                      value_out, first_value_out):
    left = lax.axis_index("transpor") < partitions // 2
    on = ready(couplings(left, hop, prev)[3]())
    source = minus(take(reduced, 2), cmul_ready(on, ready(take(carry_held, 0))))
    value = cmul_ready(ready(take(inverse, 0)), ready(source))
    put(value_out, 0, value)
    change = cmul_ready(ready(take(first, 0)), ready(value))
    put(first_value_out, 0, minus(take(first, 2), change))


def back_kernel(value, on, held, first, second_out, first_out):
    change = cmul_ready(ready(take(on, 0)), ready(take(value, 0)))
    result = minus(take(held, 0), change)
    put(second_out, 0, result)
    change = cmul_ready(ready(take(first, 0)), ready(result))
    put(first_out, 0, minus(take(first, 2), change))


def place(half, offset):
    row = lax.broadcasted_iota(jnp.int32, (half, half), 0)
    column = lax.broadcasted_iota(jnp.int32, (half, half), 1)
    return row, column


def pack(block_re, block_im):
    half = block_re.shape[0] // 2
    row, column = place(half, 0)
    top_re, top_im = block_re[:half, :half], block_im[:half, :half]
    low_re, low_im = block_re[half:, half:], block_im[half:, half:]
    both_re = jnp.where(column >= row, top_re, low_re)
    both_im = jnp.where(column > row, top_im, jnp.where(column == row, low_re, low_im))
    return (
        jnp.concatenate([both_re, block_re[:half, half:]], axis=1),
        jnp.concatenate([both_im, block_im[:half, half:]], axis=1),
    )


def unpack(packed_re, packed_im):
    half = packed_re.shape[0]
    row, column = place(half, 0)
    both_re, side_re = packed_re[:, :half], packed_re[:, half:]
    both_im, side_im = packed_im[:, :half], packed_im[:, half:]
    turned_re, turned_im = jnp.transpose(both_re), -jnp.transpose(both_im)
    top_re = jnp.where(column >= row, both_re, turned_re)
    low_re = jnp.where(column < row, both_re, jnp.where(column == row, both_im, turned_re))
    top_im = jnp.where(column > row, both_im, jnp.where(column == row, 0.0, turned_im))
    low_im = jnp.where(column < row, both_im, jnp.where(column == row, 0.0, turned_im))
    whole_re = jnp.concatenate(
        [
            jnp.concatenate([top_re, side_re], axis=1),
            jnp.concatenate([jnp.transpose(side_re), low_re], axis=1),
        ],
        axis=0,
    )
    whole_im = jnp.concatenate(
        [
            jnp.concatenate([top_im, side_im], axis=1),
            jnp.concatenate([-jnp.transpose(side_im), low_im], axis=1),
        ],
        axis=0,
    )
    return whole_re, whole_im


def fold(first, second):
    half = first.shape[0]
    return jnp.concatenate(
        [
            first[:, :LANES],
            second[:, :LANES],
            jnp.concatenate([first[:, LANES:], second[:, LANES:]], axis=1),
        ],
        axis=0,
    )


def unfold(rows_of, half):
    tail = rows_of[2 * half :]
    side = tail.shape[1] // 2
    return (
        jnp.concatenate([rows_of[:half], tail[:, :side]], axis=1),
        jnp.concatenate([rows_of[half : 2 * half], tail[:, side:]], axis=1),
    )


def exchange_kernel(count, half_way, value_a, value_b, weight, slot, polar_out,
                    packed, arrived, ordered, sums, returned, merged,
                    out_sem, in_sem, back_sem, home_sem):
    me = lax.axis_index("energy")
    left = lax.axis_index("transpor") < half_way
    order = value_a.shape[1]
    half = order // 2
    rows = sums.shape[2]
    barrier = pltpu.get_barrier_semaphore()
    for step in range(1, count):
        pl.semaphore_signal(
            barrier,
            inc=1,
            device_id={"energy": lax.rem(me + step, count)},
            device_id_type=pl.DeviceIdType.MESH,
        )
    kinds = [[], []]
    for first, second in ((value_a, value_b), (value_b, value_a)):
        state_re = jnp.where(left, first[0], second[0])
        state_im = jnp.where(left, first[1], second[1])
        turned = ready_turned((state_re, state_im))
        for kind in range(2):
            held = weight[kind : kind + 1, :]
            weighted = ready((state_re * held, state_im * held))
            kinds[kind].append(pack(*cmul_turned(weighted, turned)))
    for kind in range(2):
        for part in range(2):
            flat = fold(kinds[kind][0][part], kinds[kind][1][part])
            for piece in range(count):
                packed[piece, 2 * kind + part, :rows] = flat[piece * rows : (piece + 1) * rows]
    for piece in range(count):
        for part in range(4):
            packed[piece, part, rows:] = slot[...]
    pl.semaphore_wait(barrier, count - 1)

    def there(step):
        other = lax.rem(me + step, count)
        return pltpu.make_async_remote_copy(
            src_ref=packed.at[other],
            dst_ref=arrived.at[me],
            send_sem=out_sem.at[step],
            recv_sem=in_sem.at[step],
            device_id={"energy": other},
            device_id_type=pl.DeviceIdType.MESH,
        )

    for step in range(1, count):
        there(step).start()
    arrived[me] = packed[me]
    for step in range(1, count):
        there(step).wait_recv()

    own = me * rows + lax.broadcasted_iota(jnp.int32, (rows, LANES), 0)
    lane = lax.broadcasted_iota(jnp.int32, (rows, LANES), 1)
    within = jnp.where(own >= half, own - half, own)
    on_diagonal = (own < order) & (lane == within)
    for position in range(count):
        total = [jnp.zeros((rows, LANES), jnp.float32)] * 4
        for source in range(count):
            here = arrived[source, 0, rows:] == position
            total = [
                jnp.where(here, arrived[source, part, :rows], total[part]) for part in range(4)
            ]
        ordered[position, 0] = total[0]
        ordered[position, 1] = total[1]
        ordered[position, 2] = total[2]
        ordered[position, 3] = jnp.where(on_diagonal, 0.0, total[3])
        ordered[position, 4] = jnp.where(on_diagonal, total[3], total[2])
    for lag in range(count):
        sum_re = jnp.zeros((rows, LANES), jnp.float32)
        sum_im = jnp.zeros((rows, LANES), jnp.float32)
        for position in range(lag, count):
            before = position - lag
            lesser_re, lesser_im = ordered[position, 0], ordered[position, 1]
            greater_im = ordered[before, 3]
            sum_re = sum_re + (lesser_re * ordered[before, 2] + lesser_im * greater_im)
            sum_im = sum_im + (lesser_im * ordered[before, 4] - lesser_re * greater_im)
        sums[lag, 0] = sum_re / count
        sums[lag, 1] = sum_im / count

    def back(step):
        other = lax.rem(me + step, count)
        return pltpu.make_async_remote_copy(
            src_ref=sums.at[other],
            dst_ref=returned.at[me],
            send_sem=back_sem.at[step],
            recv_sem=home_sem.at[step],
            device_id={"energy": other},
            device_id_type=pl.DeviceIdType.MESH,
        )

    for step in range(1, count):
        back(step).start()
    returned[me] = sums[me]
    for step in range(1, count):
        back(step).wait_recv()
    for piece in range(count):
        for part in range(2):
            merged[part, piece * rows : (piece + 1) * rows] = returned[piece, part]
    parts = [unfold(merged[part], half) for part in range(2)]
    for block in range(2):
        whole_re, whole_im = unpack(parts[0][block], parts[1][block])
        polar_out[0, block, 0] = whole_re
        polar_out[0, block, 1] = whole_im
    for step in range(1, count):
        there(step).wait_send()
        back(step).wait_send()


def exchange(value_a, value_b, weight, slot, count, half_way):
    order = value_a.shape[1]
    rows = order * order // LANES // count
    dma = pltpu.SemaphoreType.DMA((count,))
    return pl.pallas_call(
        functools.partial(exchange_kernel, count, half_way),
        out_shape=jax.ShapeDtypeStruct((1, 2, 2, order, order), jnp.float32),
        scratch_shapes=[
            pltpu.VMEM((count, 4, rows + 1, LANES), jnp.float32),
            pltpu.VMEM((count, 4, rows + 1, LANES), jnp.float32),
            pltpu.VMEM((count, 5, rows, LANES), jnp.float32),
            pltpu.VMEM((count, 2, rows, LANES), jnp.float32),
            pltpu.VMEM((count, 2, rows, LANES), jnp.float32),
            pltpu.VMEM((2, rows * count, LANES), jnp.float32),
            dma,
            dma,
            dma,
            dma,
        ],
        compiler_params=pltpu.CompilerParams(
            collective_id=0, has_side_effects=True, vmem_limit_bytes=48 * 1024 * 1024
        ),
    )(value_a, value_b, weight, slot)


def call(body, counts, order, scratch=True, inverses=0):
    shapes = [jax.ShapeDtypeStruct((count, order, order), jnp.float32) for count in counts]
    return pl.pallas_call(
        body,
        out_shape=shapes,
        scratch_shapes=[pltpu.VMEM((2, order, order), jnp.float32)] if scratch else [],
        compiler_params=pltpu.CompilerParams(vmem_limit_bytes=48 * 1024 * 1024),
        cost_estimate=pl.CostEstimate(
            flops=(4 + 22 * inverses) * 18 * order**3,
            bytes_accessed=64 * order**2,
            transcendentals=0,
        ),
    )


def passed_along(x, axis, by):
    length = lax.axis_size(axis)
    pairs = [(i, i + by) for i in range(length) if 0 <= i + by < length]
    return lax.ppermute(x, axis, pairs)


def per_device(ham_diag, ham_hop, inject, chemical, energy_slot, onsite_shift, onsite_loss):
    orbitals = ham_diag.shape[2]
    energies = energy_slot.shape[0]
    partitions = lax.axis_size("transpor")
    half = partitions // 2
    my_index = lax.axis_index("transpor")
    grid_total = energies * lax.axis_size("energy")
    energy = ENERGY_LOW + ENERGY_SPAN * (energy_slot.astype(jnp.float32) + 0.5) / grid_total
    prev_hop = passed_along(ham_hop[-1], "transpor", 1)
    levels = jnp.full((1, orbitals), energy[0])
    shift, loss = onsite_shift[0], onsite_loss[0]

    four = jnp.zeros((4, orbitals, orbitals), jnp.float32)
    two = jnp.zeros((2, orbitals, orbitals), jnp.float32)
    carry_on = carry_held = two
    kept = (four, two, two, four)
    for stage in range(half):
        active = (my_index == stage) | (my_index == partitions - 1 - stage)
        body = functools.partial(eliminate_kernel, stage == 0, partitions)
        eliminate = call(body, (4, 2, 2, 4), orbitals, inverses=2)
        kept = lax.cond(
            active,
            lambda on, held, then, eliminate=eliminate: tuple(
                eliminate(on, held, ham_diag, ham_hop, prev_hop, inject, shift, loss, levels)
            ),
            lambda on, held, then: then,
            carry_on,
            carry_held,
            kept,
        )
        other = partitions - 1 - stage
        if stage < half - 1:
            pairs = [(stage, stage + 1), (other, other - 1)]
        else:
            pairs = [(stage, other), (other, stage)]
        carry_on = lax.ppermute(kept[1], "transpor", pairs)
        sent = kept[2]
        if stage == half - 1:
            carry_on, sent = lax.optimization_barrier((carry_on, sent))
        carry_held = lax.ppermute(sent, "transpor", pairs)
    first, on, held, reduced = kept
    join_inverse = call(
        functools.partial(join_inverse_kernel, partitions), (2,), orbitals, inverses=1
    )
    join_value = call(functools.partial(join_value_kernel, partitions), (2, 2), orbitals, False)
    (inverse,) = join_inverse(carry_on, reduced, ham_hop, prev_hop)
    value_b, value_a = join_value(carry_held, inverse, reduced, first, ham_hop, prev_hop)
    for stage in range(half - 2, -1, -1):
        other = partitions - 1 - stage
        passed = lax.ppermute(value_a, "transpor", [(stage + 1, stage), (other - 1, other)])
        new_b, new_a = call(back_kernel, (2, 2), orbitals, False)(passed, on, held, first)
        active = (my_index == stage) | (my_index == other)
        value_b = jnp.where(active, new_b, value_b)
        value_a = jnp.where(active, new_a, value_a)
    occupied = 1.0 / (1.0 + jnp.exp((energy[0] - chemical[None, :]) / THERMAL))
    weight = jnp.concatenate([occupied, 1.0 - occupied], axis=0)
    slot = jnp.full((1, LANES), energy_slot[0].astype(jnp.float32))
    return exchange(value_a, value_b, weight, slot, grid_total, half)


def solution(mesh):
    in_specs = (
        P("transpor", None, None, None),
        P("transpor", None, None, None),
        P("transpor", None, None, None),
        P(),
        P("energy"),
        P("energy", "transpor", None),
        P("energy", "transpor", None),
    )
    out_specs = P("energy", "transpor", None, None, None)
    return jax.shard_map(
        per_device, mesh=mesh, in_specs=in_specs, out_specs=out_specs, check_vma=False
    )
```
